32 devices in a mesh: row: 8 (over z, x), col: 4 (over y, core).
Axes of the slice: x: 2, y: 2, z: 4, core: 2. Of those that a mesh axis runs over, the one named last changes fastest.
Arguments:
- source_points: float32 [3, 16384], P(None, 'row'), may hold values from -4 to 4
- target_points: float32 [3, 65536], P(None, 'col'), may hold values from -4 to 4
- source_potential: float32 [16384], P('row'), may hold values from -2.5 to 3.6
- target_potential: float32 [65536], P('col'), may hold values from -2.5 to 3.6
- neighbours: int32 [64, 64], P('row'), may hold values from -1 to 255, as said below
Outputs:
- source_dual: float32 [16384], P('row')
- target_dual: float32 [65536], P('col')
The draws below stay inside these ranges and needn't reach their ends.
Inputs may be any that keep to these rules, and one draw needn't show every extreme that they name: `neighbours`: each row block lists, in increasing order, between 32 and 64 distinct column-block ids, then -1 up to 64 entries; some row block lists 64; every column block is listed by at least one row block.
All inputs are finite; a program needn't handle non-finite values.
Results may differ from the reference program's by a relative error of at most 0.0003.
Values sent between devices are 32-bit elements; how exact they have to be, the bound alone decides.
A program may use at most 64 MiB of HBM per device.

```python
import jax
import jax.numpy as jnp
from jax import lax

BLOCK = 256
NBR_MOST = 64
ITERS = 2
CB_DEV = 64
ROW_BLOCKS = 64
COL_BLOCKS = 256
SOURCES = 16384
TARGETS = 65536
N_COL = 4


def potential_values(key, amount):
    values = 0.5 * jax.random.normal(key, (amount,), jnp.float32)
    return jnp.clip(values, -2.5, 2.5).astype(jnp.float32)


def draw_source_potential(key, part):
    return potential_values(jax.random.fold_in(key, 11), SOURCES)


def draw_target_potential(key, part):
    return potential_values(jax.random.fold_in(key, 23), TARGETS)


def draw_neighbours(key, part):
    first, second, third, fourth = jax.random.split(jax.random.fold_in(key, 37), 4)
    columns = jnp.arange(COL_BLOCKS, dtype=jnp.int32)
    row_ids = jnp.arange(ROW_BLOCKS, dtype=jnp.int32)
    owner_weight = jax.random.randint(first, (N_COL,), 0, 4, dtype=jnp.int32) * 8192
    noise = jax.random.randint(second, (ROW_BLOCKS, COL_BLOCKS), 0, 16384, dtype=jnp.int32)
    scores = noise + owner_weight[columns // CB_DEV][None, :]
    period = min(ROW_BLOCKS, COL_BLOCKS)
    forced = columns[None, :] % period == row_ids[:, None] % period
    scores = jnp.where(forced, scores + 65536, scores)
    scores = scores * COL_BLOCKS + columns[None, :]
    unused, picked = lax.top_k(scores, NBR_MOST)
    lengths = jax.random.randint(third, (ROW_BLOCKS,), NBR_MOST // 2, NBR_MOST + 1, dtype=jnp.int32)
    full_row = jax.random.randint(fourth, (), 0, ROW_BLOCKS, dtype=jnp.int32)
    lengths = jnp.where(row_ids == full_row, NBR_MOST, lengths)
    keep = jnp.arange(NBR_MOST, dtype=jnp.int32)[None, :] < lengths[:, None]
    listed = jnp.where(keep, picked.astype(jnp.int32), COL_BLOCKS)
    listed = jnp.sort(listed, axis=1)
    return jnp.where(listed == COL_BLOCKS, -1, listed).astype(jnp.int32)


def block_scale(rng, extent, pieces, least, largest):
    def one(axis_at, blocks):
        steps = jax.random.uniform(jax.random.fold_in(jax.random.fold_in(rng, 6), axis_at), (blocks,), jnp.float32, least / len(pieces), largest / len(pieces))
        return jnp.repeat(jnp.exp(steps), extent[axis_at] // blocks).reshape((-1,) + (1,) * (len(extent) - axis_at - 1))

    gain = one(*pieces[0])
    for cut in pieces[1:]:
        gain = gain * one(*cut)
    return gain


def bell_draw(own_key, shape, scale, most, pieces=(), kind=jnp.bfloat16):
    array = jax.random.normal(own_key, shape, jnp.float32) * scale
    if len(pieces) > 0:
        array = block_scale(own_key, shape, pieces, -0.22, 0.18) * array
    return jnp.clip(array, min=-most, max=most).astype(kind)


def setup_inputs(seed: int = 0) -> dict:
    splits = jax.random.split(jax.random.key(seed), 6)
    source_points = bell_draw(splits[0], (3, SOURCES), 1.0, 4.0, ((1, 8),), jnp.float32)
    target_points = bell_draw(splits[1], (3, TARGETS), 1.0, 4.0, ((1, 4),), jnp.float32)
    source_potential = draw_source_potential(jax.random.fold_in(splits[5], 71), 0)
    target_potential = draw_target_potential(jax.random.fold_in(splits[5], 71), 0)
    neighbours = draw_neighbours(jax.random.fold_in(splits[5], 71), 0)
    return {"source_points": source_points, "target_points": target_points, "source_potential": source_potential, "target_potential": target_potential, "neighbours": neighbours}


EPS = 0.02


def block_terms(packed, target_grid, target_level):
    source_block, source_level, listed_ids, listed = packed
    target_pick = target_grid[:, listed_ids]
    level_pick = target_level[listed_ids]
    first = source_block[0][:, None, None] - target_pick[0][None]
    second = source_block[1][:, None, None] - target_pick[1][None]
    third = source_block[2][:, None, None] - target_pick[2][None]
    pair_cost = 0.5 * (first * first + second * second + third * third)
    row_score = (level_pick[None] - pair_cost) / EPS
    row_score = jnp.where(listed[None, :, None], row_score, -jnp.inf)
    row_top = jnp.max(row_score, axis=(1, 2))
    row_mass = jnp.sum(jnp.exp(row_score - row_top[:, None, None]), axis=(1, 2))
    row_update = -EPS * (row_top + jnp.log(row_mass))
    col_score = (source_level[:, None, None] - pair_cost) / EPS
    col_top = jnp.max(col_score, axis=0)
    col_mass = jnp.sum(jnp.exp(col_score - col_top[None]), axis=0)
    col_top = jnp.where(listed[:, None], col_top, -jnp.inf)
    col_mass = jnp.where(listed[:, None], col_mass, jnp.zeros_like(col_mass))
    return row_update, col_top, col_mass


def reference(source_points, target_points, source_potential, target_potential, neighbours):
    source_grid = source_points.reshape(3, ROW_BLOCKS, BLOCK).transpose(1, 0, 2)
    target_grid = target_points.reshape(3, COL_BLOCKS, BLOCK)
    listed = neighbours >= 0
    listed_ids = jnp.where(listed, neighbours, 0).astype(jnp.int32)
    segment_ids = jnp.where(listed, neighbours, COL_BLOCKS).astype(jnp.int32).reshape(-1)
    source_dual = source_potential
    target_dual = target_potential
    for sweep in range(ITERS):
        source_level = source_dual.reshape(ROW_BLOCKS, BLOCK)
        target_level = target_dual.reshape(COL_BLOCKS, BLOCK)

        def per_block(packed):
            return block_terms(packed, target_grid, target_level)

        row_update, col_top, col_mass = lax.map(per_block, (source_grid, source_level, listed_ids, listed))
        col_top = col_top.reshape(-1, BLOCK)
        col_mass = col_mass.reshape(-1, BLOCK)
        column_peak = jax.ops.segment_max(col_top, segment_ids, num_segments=COL_BLOCKS + 1)
        column_peak = column_peak.at[COL_BLOCKS].set(jnp.zeros((BLOCK,), column_peak.dtype))
        shifted = col_mass * jnp.exp(col_top - column_peak[segment_ids])
        column_mass = jax.ops.segment_sum(shifted, segment_ids, num_segments=COL_BLOCKS + 1)
        col_update = -EPS * (column_peak[:COL_BLOCKS] + jnp.log(column_mass[:COL_BLOCKS]))
        source_dual = 0.5 * (source_dual + row_update.reshape(-1))
        target_dual = 0.5 * (target_dual + col_update.reshape(-1))
    return source_dual, target_dual
```

```python
import functools
import math

import jax
import jax.numpy as jnp
from jax import lax
from jax.experimental import pallas as pl
from jax.experimental.pallas import tpu as pltpu
from jax.sharding import PartitionSpec as P

BLOCK = 256
ITERS = 2
EPS = 0.02
SCALE = math.log2(math.e) / EPS
NEG = -1e30
UNROLL = 4
DEPTH = 48
VMEM = pltpu.VMEM
SMEM = pltpu.SMEM


def pieces(values):
    first = values.astype(jnp.bfloat16).astype(jnp.float32)
    rest = values - first
    second = rest.astype(jnp.bfloat16).astype(jnp.float32)
    return first, second, rest - second


def augmented(points, level, source):
    packed = jnp.concatenate([points, points], axis=0)
    place = lax.broadcasted_iota(jnp.int32, packed.shape, 0)
    squares = jnp.where(place < 3, packed * packed, 0.0)
    norm = jnp.sum(squares, axis=0, keepdims=True)
    level = SCALE * (level - 0.5 * norm)
    if source:
        level_at, one_at, coordinates = 3, 4, SCALE * packed
    else:
        level_at, one_at, coordinates = 4, 3, packed
    rows = jnp.where(
        place < 3,
        coordinates,
        jnp.where(place == level_at, level, jnp.where(place == one_at, 1.0, 0.0)),
    )
    a, b, c = pieces(rows)
    if source:
        return jnp.concatenate([a, a, b, b, a, c], axis=0)
    return jnp.concatenate([a, b, a, b, c, a], axis=0)


def slot_lse(scores):
    tiles = scores.reshape(scores.shape[0] // 8, 8, scores.shape[1])
    top = jnp.max(tiles, axis=0)
    return top, jnp.sum(jnp.exp2(tiles - top[None]), axis=0)


def merge(top_ref, mass_ref, at, top, mass):
    old = top_ref[at]
    new = jnp.maximum(old, top)
    top_ref[at] = new
    mass_ref[at] = mass_ref[at] * jnp.exp2(old - new) + mass * jnp.exp2(top - new)


def total(top, mass):
    peak = jnp.max(top, axis=1)
    amount = jnp.sum(mass * jnp.exp2(top - peak[:, None, :]), axis=1)
    return peak + jnp.log2(jnp.maximum(amount, 1e-30))


def sweep_kernel(
    count, row_list, col_list, source, f, target, g, row_out, g_out,
    x_all, xt_all, y_all, yt_all, row_top, row_mass, col_top, col_mass,
):
    rows, cols = f.shape[0], g.shape[0]

    def build(at, ref, level, straight, turned, is_source):
        per = ref.shape[2] // BLOCK
        lanes = pl.ds(pl.multiple_of(at % per * BLOCK, BLOCK), BLOCK)
        block = augmented(ref[at // per, :, lanes], level[at], is_source)
        turned[at] = block.astype(jnp.bfloat16)
        straight[at] = block.T.astype(jnp.bfloat16)

    @pl.loop(0, rows, unroll=4)
    def _(at):
        build(at, source, f, x_all, xt_all, True)

    for at in range(cols):
        build(at, target, g, y_all, yt_all, False)
    x_all[rows] = jnp.zeros_like(x_all[rows])
    xt_all[rows] = jnp.zeros_like(xt_all[rows])
    y_all[cols] = jnp.zeros_like(y_all[cols])
    yt_all[cols] = jnp.zeros_like(yt_all[cols])
    row_top[...] = jnp.full_like(row_top, NEG)
    row_mass[...] = jnp.zeros_like(row_mass)
    col_top[...] = jnp.full_like(col_top, NEG)
    col_mass[...] = jnp.zeros_like(col_mass)

    @pl.loop(0, (count[0] + UNROLL - 1) // UNROLL)
    def _(turn):
        found = []
        for lane in range(UNROLL):
            row = row_list[turn * UNROLL + lane]
            col = col_list[turn * UNROLL + lane]
            by_col = jnp.dot(x_all[row], yt_all[col], preferred_element_type=jnp.float32)
            by_row = jnp.dot(y_all[col], xt_all[row], preferred_element_type=jnp.float32)
            found.append((row, col, slot_lse(by_row), slot_lse(by_col)))
        for row, col, of_row, of_col in found:
            merge(row_top, row_mass, row, *of_row)
            merge(col_top, col_mass, col, *of_col)

    row_out[...] = total(row_top[:rows], row_mass[:rows])
    g_out[...] = g[:, 0, :] - total(col_top[:cols], col_mass[:cols]) / (2 * SCALE)


def sweep(count, row_list, col_list, source, f, target, g):
    f, g = f.reshape(-1, 1, BLOCK), g.reshape(-1, 1, BLOCK)
    rows, cols = f.shape[0], g.shape[0]
    bf16, f32 = jnp.bfloat16, jnp.float32
    return pl.pallas_call(
        sweep_kernel,
        out_shape=(
            jax.ShapeDtypeStruct((rows, BLOCK), f32),
            jax.ShapeDtypeStruct((cols, BLOCK), f32),
        ),
        in_specs=[pl.BlockSpec(memory_space=SMEM)] * 3 + [pl.BlockSpec(memory_space=VMEM)] * 4,
        out_specs=(pl.BlockSpec(memory_space=VMEM),) * 2,
        scratch_shapes=[
            VMEM((rows + 1, BLOCK, DEPTH), bf16),
            VMEM((rows + 1, DEPTH, BLOCK), bf16),
            VMEM((cols + 1, BLOCK, DEPTH), bf16),
            VMEM((cols + 1, DEPTH, BLOCK), bf16),
            VMEM((rows + 1, 8, BLOCK), f32),
            VMEM((rows + 1, 8, BLOCK), f32),
            VMEM((cols + 1, 8, BLOCK), f32),
            VMEM((cols + 1, 8, BLOCK), f32),
        ],
        compiler_params=pltpu.CompilerParams(vmem_limit_bytes=48 * 1024 * 1024),
    )(count, row_list, col_list, source, f, target, g)


def lse2(parts):
    peak = jnp.max(parts, axis=0)
    return peak + jnp.log2(jnp.sum(jnp.exp2(parts - peak[None]), axis=0))


def place_of(device, n_col):
    return (device // n_col, lax.rem(device, n_col))


def meet(peers):
    barrier = pltpu.get_barrier_semaphore()
    for amount, where in peers:

        @pl.loop(1, amount)
        def _(step):
            pl.semaphore_signal(
                barrier, inc=1, device_id=where(step), device_id_type=pl.DeviceIdType.MESH
            )

    pl.semaphore_wait(barrier, sum(amount - 1 for amount, _ in peers))


def remote(src, dst, send, recv, where):
    return pltpu.make_async_remote_copy(
        src_ref=src, dst_ref=dst, send_sem=send, recv_sem=recv,
        device_id=where, device_id_type=pl.DeviceIdType.MESH,
    )


def gather_kernel(
    n_row, n_col, spread, source, lists, target, source_out, lists_out, target_out,
    source_send, source_recv, lists_send, lists_recv, target_send, target_recv,
):
    row, col = lax.axis_index("row"), lax.axis_index("col")

    def by_row(step):
        return (lax.rem(row + step, n_row), col)

    def by_col(step):
        return (row, lax.rem(col + step, n_col))

    meet([(n_row, by_row)] + ([(n_col, by_col)] if spread else []))

    def copies(step):
        to = by_row(step)
        return (
            remote(source, source_out.at[row], source_send.at[step], source_recv.at[step], to),
            remote(lists, lists_out.at[row], lists_send.at[step], lists_recv.at[step], to),
        )

    def target_copy(step):
        to = by_col(step)
        return remote(
            target.at[to[1]], target_out.at[col], target_send.at[step], target_recv.at[step], to
        )

    @pl.loop(1, n_row)
    def _(step):
        for copy in copies(step):
            copy.start()

    if spread:

        @pl.loop(1, n_col)
        def _(step):
            target_copy(step).start()

        target_out[col] = target[col]

        @pl.loop(1, n_col)
        def _(step):
            target_copy(step).wait()
    else:
        target_out[...] = target[...]

    source_out[row] = source[...]
    lists_out[row] = lists[...]

    @pl.loop(1, n_row)
    def _(step):
        for copy in copies(step):
            copy.wait()


def gather(n_row, n_col, spread, source, lists, target):
    dma = pltpu.SemaphoreType.DMA
    return pl.pallas_call(
        functools.partial(gather_kernel, n_row, n_col, spread),
        out_shape=(
            jax.ShapeDtypeStruct((n_row,) + source.shape, source.dtype),
            jax.ShapeDtypeStruct((n_row,) + lists.shape, lists.dtype),
            jax.ShapeDtypeStruct(target.shape, target.dtype),
        ),
        in_specs=[pl.BlockSpec(memory_space=VMEM)] * 3,
        out_specs=(pl.BlockSpec(memory_space=VMEM),) * 3,
        scratch_shapes=[dma((n_row,))] * 4 + [dma((n_col,))] * 2,
        compiler_params=pltpu.CompilerParams(
            collective_id=0, has_side_effects=True, vmem_limit_bytes=32 * 1024 * 1024
        ),
    )(source, lists, target)


def exchange_kernel(n_row, n_col, spread, last, *refs):
    if last:
        (
            sums, f, g, f_out, g_out,
            parts, send, recv, f_send, f_recv, g_send, g_recv,
        ) = refs
    else:
        sums, f, f_out, parts, send, recv, f_send, f_recv = refs
    n_dev = n_row * n_col
    row, col = lax.axis_index("row"), lax.axis_index("col")
    me = row * n_col + col

    def anyone(step):
        return place_of(lax.rem(me + step, n_dev), n_col)

    def by_col(step):
        return (row, lax.rem(col + step, n_col))

    def by_row(step):
        return (lax.rem(row + step, n_row), col)

    meet([(n_dev, anyone)])

    def sum_copy(step):
        return remote(
            sums.at[lax.rem(me + step, n_dev)], parts.at[me],
            send.at[step], recv.at[step], anyone(step),
        )

    def g_copy(step):
        to = anyone(step) if spread else by_row(step)
        return remote(
            g.at[to[1] if spread else 0], g_out.at[me if spread else row],
            g_send.at[step], g_recv.at[step], to,
        )

    @pl.loop(1, n_dev)
    def _(step):
        sum_copy(step).start()

    parts[me] = sums[me]
    if last:

        @pl.loop(1, n_dev if spread else n_row)
        def _(step):
            g_copy(step).start()

        g_out[me if spread else row] = g[col if spread else 0]

    @pl.loop(1, n_dev)
    def _(step):
        sum_copy(step).wait()

    spot = col if last else me
    f_out[spot] = f[me] - lse2(parts[...]) / (2 * SCALE)
    amount, where = (n_col, by_col) if last else (n_dev, anyone)

    def f_copy(step):
        return remote(
            f_out.at[spot], f_out.at[spot], f_send.at[step], f_recv.at[step], where(step)
        )

    @pl.loop(1, amount)
    def _(step):
        f_copy(step).start()

    if last:

        @pl.loop(1, n_dev if spread else n_row)
        def _(step):
            g_copy(step).wait()

    @pl.loop(1, amount)
    def _(step):
        f_copy(step).wait()


def exchange(n_row, n_col, spread, last, sums, f, g):
    n_dev = n_row * n_col
    dma = pltpu.SemaphoreType.DMA
    sums, f = (a.reshape(n_dev, -1, 128) for a in (sums, f))
    amount = n_col if last else n_dev
    out = [jax.ShapeDtypeStruct((amount,) + f.shape[1:], f.dtype)]
    scratch = [VMEM(sums.shape, sums.dtype)] + [dma((n_dev,))] * 2 + [dma((amount,))] * 2
    args = [sums, f]
    if last:
        fan = n_dev if spread else n_row
        g = g.reshape(n_col if spread else 1, -1, 128)
        out.append(jax.ShapeDtypeStruct((fan,) + g.shape[1:], g.dtype))
        scratch += [dma((fan,))] * 2
        args.append(g)
    return pl.pallas_call(
        functools.partial(exchange_kernel, n_row, n_col, spread, last),
        out_shape=tuple(out),
        in_specs=[pl.BlockSpec(memory_space=VMEM)] * len(args),
        out_specs=(pl.BlockSpec(memory_space=VMEM),) * len(out),
        scratch_shapes=scratch,
        compiler_params=pltpu.CompilerParams(
            collective_id=2 if last else 1,
            has_side_effects=True,
            vmem_limit_bytes=32 * 1024 * 1024,
        ),
    )(*args)


def on_device(n_row, n_col, source_points, target_points, source_level, target_level, neighbours):
    group = target_points.shape[1] // BLOCK
    share = group // n_row
    spread = share % n_col == 0
    me_row, me_col = lax.axis_index("row"), lax.axis_index("col")
    start, length = me_row * share * BLOCK, share * BLOCK
    source = jnp.concatenate([source_points, source_level[None]], axis=0)
    target = jnp.concatenate(
        [
            lax.dynamic_slice_in_dim(target_points, start, length, 1),
            lax.dynamic_slice_in_dim(target_level, start, length, 0)[None],
        ],
        axis=0,
    )
    if spread:
        target = target.reshape(4, n_col, -1).transpose(1, 0, 2)
        part = share // n_col
        own = (
            jnp.arange(n_col)[:, None] * group
            + me_row * share + me_col * part + jnp.arange(part)[None, :]
        ).reshape(-1)
    else:
        target = target[None]
        own = me_col * group + me_row * share + jnp.arange(share)
    source, lists, target = gather(n_row, n_col, spread, source, neighbours, target)
    lists = lists.reshape(-1, lists.shape[-1])
    f, g = source[:, 3], target[:, 3]
    rows = lists.shape[0]
    cols = own.shape[0]
    capacity = rows * cols
    mask = jnp.any(lists[None] == own[:, None, None], axis=2).reshape(-1)
    order = jnp.arange(capacity)
    place = jnp.sum(jnp.where((order[None, :] <= order[:, None]) & mask[None, :], 1, 0), axis=1)
    count = place[-1:]
    hit = mask[None, :] & (place[None, :] == order[:, None] + 1)
    pick = jnp.sum(jnp.where(hit, order[None, :], 0), axis=1)
    live = order < count
    row_list = jnp.where(live, pick % rows, rows)
    col_list = jnp.where(live, pick // rows, cols)

    for turn in range(ITERS):
        sums, g = sweep(count, row_list, col_list, source, f, target, g)
        if turn < ITERS - 1:
            (f,) = exchange(n_row, n_col, spread, False, sums, f, None)
    f, g = exchange(n_row, n_col, spread, True, sums, f, g)
    return f.reshape(-1), g.reshape(-1)


def solution(mesh):
    return jax.shard_map(
        functools.partial(on_device, mesh.shape["row"], mesh.shape["col"]),
        mesh=mesh,
        in_specs=(P(None, "row"), P(None, "col"), P("row"), P("col"), P("row", None)),
        out_specs=(P("row"), P("col")),
        check_vma=False,
    )
```

```python
import functools
import math

import jax
import jax.numpy as jnp
from jax import lax
from jax.experimental import pallas as pl
from jax.experimental.pallas import tpu as pltpu
from jax.sharding import PartitionSpec as P

BLOCK = 256
ITERS = 2
EPS = 0.02
SCALE = math.log2(math.e) / EPS
NEG = -1e30
UNROLL = 8
CUT = 4
DEPTH = 48
VMEM = pltpu.VMEM
SMEM = pltpu.SMEM


def pieces(values):
    first = values.astype(jnp.bfloat16).astype(jnp.float32)
    rest = values - first
    second = rest.astype(jnp.bfloat16).astype(jnp.float32)
    return first, second, rest - second


def augmented(points, level, source):
    packed = jnp.concatenate([points, points], axis=0)
    place = lax.broadcasted_iota(jnp.int32, packed.shape, 0)
    squares = jnp.where(place < 3, packed * packed, 0.0)
    norm = jnp.sum(squares, axis=0, keepdims=True)
    level = SCALE * (level - 0.5 * norm)
    if source:
        level_at, one_at, coordinates = 3, 4, SCALE * packed
    else:
        level_at, one_at, coordinates = 4, 3, packed
    rows = jnp.where(
        place < 3,
        coordinates,
        jnp.where(place == level_at, level, jnp.where(place == one_at, 1.0, 0.0)),
    )
    a, b, c = pieces(rows)
    if source:
        return jnp.concatenate([a, a, b, b, a, c], axis=0)
    return jnp.concatenate([a, b, a, b, c, a], axis=0)


def slot_lse(scores):
    depth = scores.shape[0] // CUT
    tops, masses = [], []
    for at in range(CUT):
        tiles = scores[at * depth : (at + 1) * depth].reshape(depth // 8, 8, scores.shape[1])
        top = jnp.max(tiles, axis=0)
        tops.append(top)
        masses.append(jnp.sum(jnp.exp2(tiles - top[None]), axis=0))
    peak = functools.reduce(jnp.maximum, tops)
    return peak, sum(mass * jnp.exp2(top - peak) for top, mass in zip(tops, masses))


def merge(top_ref, mass_ref, at, top, mass):
    old = top_ref[at]
    new = jnp.maximum(old, top)
    top_ref[at] = new
    mass_ref[at] = mass_ref[at] * jnp.exp2(old - new) + mass * jnp.exp2(top - new)


def total(top, mass):
    peak = jnp.max(top, axis=1)
    amount = jnp.sum(mass * jnp.exp2(top - peak[:, None, :]), axis=1)
    return peak + jnp.log2(jnp.maximum(amount, 1e-30))


def sweep_kernel(
    pairs, source, f, target, g, row_out, g_out,
    x_all, xt_all, y_all, yt_all, row_top, row_mass, col_top, col_mass,
):
    rows, cols = f.shape[0], g.shape[0]

    def build(at, ref, level, straight, turned, is_source):
        per = ref.shape[2] // BLOCK
        lanes = pl.ds(pl.multiple_of(at % per * BLOCK, BLOCK), BLOCK)
        block = augmented(ref[at // per, :, lanes], level[at], is_source)
        turned[at] = block.astype(jnp.bfloat16)
        straight[at] = block.T.astype(jnp.bfloat16)

    @pl.loop(0, rows, unroll=4)
    def _(at):
        build(at, source, f, x_all, xt_all, True)

    for at in range(cols):
        build(at, target, g, y_all, yt_all, False)
    x_all[rows] = jnp.zeros_like(x_all[rows])
    xt_all[rows] = jnp.zeros_like(xt_all[rows])
    y_all[cols] = jnp.zeros_like(y_all[cols])
    yt_all[cols] = jnp.zeros_like(yt_all[cols])
    row_top[...] = jnp.full_like(row_top, NEG)
    row_mass[...] = jnp.zeros_like(row_mass)
    col_top[...] = jnp.full_like(col_top, NEG)
    col_mass[...] = jnp.zeros_like(col_mass)

    @pl.loop(0, (pairs[pairs.shape[0] - 1] + UNROLL - 1) // UNROLL)
    def _(turn):
        found = []
        for lane in range(UNROLL):
            pair = pairs[turn * UNROLL + lane]
            row, col = pair & 0xFFFF, pair >> 16
            by_col = jnp.dot(x_all[row], yt_all[col], preferred_element_type=jnp.float32)
            by_row = jnp.dot(y_all[col], xt_all[row], preferred_element_type=jnp.float32)
            found.append((row, col, slot_lse(by_row), slot_lse(by_col)))
        for row, col, of_row, of_col in found:
            merge(row_top, row_mass, row, *of_row)
            merge(col_top, col_mass, col, *of_col)

    row_out[...] = total(row_top[:rows], row_mass[:rows])
    g_out[...] = g[:, 0, :] - total(col_top[:cols], col_mass[:cols]) / (2 * SCALE)


def sweep(pairs, source, f, target, g):
    f, g = f.reshape(-1, 1, BLOCK), g.reshape(-1, 1, BLOCK)
    rows, cols = f.shape[0], g.shape[0]
    bf16, f32 = jnp.bfloat16, jnp.float32
    return pl.pallas_call(
        sweep_kernel,
        out_shape=(
            jax.ShapeDtypeStruct((rows, BLOCK), f32),
            jax.ShapeDtypeStruct((cols, BLOCK), f32),
        ),
        in_specs=[pl.BlockSpec(memory_space=SMEM)] + [pl.BlockSpec(memory_space=VMEM)] * 4,
        out_specs=(pl.BlockSpec(memory_space=VMEM),) * 2,
        scratch_shapes=[
            VMEM((rows + 1, BLOCK, DEPTH), bf16),
            VMEM((rows + 1, DEPTH, BLOCK), bf16),
            VMEM((cols + 1, BLOCK, DEPTH), bf16),
            VMEM((cols + 1, DEPTH, BLOCK), bf16),
            VMEM((rows + 1, 8, BLOCK), f32),
            VMEM((rows + 1, 8, BLOCK), f32),
            VMEM((cols + 1, 8, BLOCK), f32),
            VMEM((cols + 1, 8, BLOCK), f32),
        ],
        compiler_params=pltpu.CompilerParams(vmem_limit_bytes=48 * 1024 * 1024),
    )(pairs, source, f, target, g)


def lse2(parts):
    peak = jnp.max(parts, axis=0)
    return peak + jnp.log2(jnp.sum(jnp.exp2(parts - peak[None]), axis=0))


def place_of(device, n_col):
    return (device // n_col, lax.rem(device, n_col))


def meet(peers):
    barrier = pltpu.get_barrier_semaphore()
    for amount, where in peers:

        @pl.loop(1, amount)
        def _(step):
            pl.semaphore_signal(
                barrier, inc=1, device_id=where(step), device_id_type=pl.DeviceIdType.MESH
            )

    pl.semaphore_wait(barrier, sum(amount - 1 for amount, _ in peers))


def remote(src, dst, send, recv, where):
    return pltpu.make_async_remote_copy(
        src_ref=src, dst_ref=dst, send_sem=send, recv_sem=recv,
        device_id=where, device_id_type=pl.DeviceIdType.MESH,
    )


def gather_kernel(
    n_row, n_col, spread, source, lists, target, source_out, lists_out, target_out,
    source_send, source_recv, lists_send, lists_recv, target_send, target_recv,
):
    row, col = lax.axis_index("row"), lax.axis_index("col")

    def by_row(step):
        return (lax.rem(row + step, n_row), col)

    def by_col(step):
        return (row, lax.rem(col + step, n_col))

    meet([(n_row, by_row)] + ([(n_col, by_col)] if spread else []))

    def copies(step):
        to = by_row(step)
        return (
            remote(source, source_out.at[row], source_send.at[step], source_recv.at[step], to),
            remote(lists, lists_out.at[row], lists_send.at[step], lists_recv.at[step], to),
        )

    def target_copy(step):
        to = by_col(step)
        return remote(
            target.at[to[1]], target_out.at[col], target_send.at[step], target_recv.at[step], to
        )

    @pl.loop(1, n_row)
    def _(step):
        for copy in copies(step):
            copy.start()

    if spread:

        @pl.loop(1, n_col)
        def _(step):
            target_copy(step).start()

        target_out[col] = target[col]

        @pl.loop(1, n_col)
        def _(step):
            target_copy(step).wait()
    else:
        target_out[...] = target[...]

    source_out[row] = source[...]
    lists_out[row] = lists[...]

    @pl.loop(1, n_row)
    def _(step):
        for copy in copies(step):
            copy.wait()


def gather(n_row, n_col, spread, source, lists, target):
    dma = pltpu.SemaphoreType.DMA
    return pl.pallas_call(
        functools.partial(gather_kernel, n_row, n_col, spread),
        out_shape=(
            jax.ShapeDtypeStruct((n_row,) + source.shape, source.dtype),
            jax.ShapeDtypeStruct((n_row,) + lists.shape, lists.dtype),
            jax.ShapeDtypeStruct(target.shape, target.dtype),
        ),
        in_specs=[pl.BlockSpec(memory_space=VMEM)] * 3,
        out_specs=(pl.BlockSpec(memory_space=VMEM),) * 3,
        scratch_shapes=[dma((n_row,))] * 4 + [dma((n_col,))] * 2,
        compiler_params=pltpu.CompilerParams(
            collective_id=0, has_side_effects=True, vmem_limit_bytes=32 * 1024 * 1024
        ),
    )(source, lists, target)


def exchange_kernel(n_row, n_col, spread, last, *refs):
    if last:
        (
            sums, f, g, f_out, g_out,
            parts, send, recv, f_send, f_recv, g_send, g_recv,
        ) = refs
    else:
        sums, f, f_out, parts, send, recv, f_send, f_recv = refs
    n_dev = n_row * n_col
    row, col = lax.axis_index("row"), lax.axis_index("col")
    me = row * n_col + col

    def anyone(step):
        return place_of(lax.rem(me + step, n_dev), n_col)

    def by_col(step):
        return (row, lax.rem(col + step, n_col))

    def by_row(step):
        return (lax.rem(row + step, n_row), col)

    meet([(n_dev, anyone)])

    def sum_copy(step):
        return remote(
            sums.at[lax.rem(me + step, n_dev)], parts.at[me],
            send.at[step], recv.at[step], anyone(step),
        )

    def g_copy(step):
        to = anyone(step) if spread else by_row(step)
        return remote(
            g.at[to[1] if spread else 0], g_out.at[me if spread else row],
            g_send.at[step], g_recv.at[step], to,
        )

    @pl.loop(1, n_dev)
    def _(step):
        sum_copy(step).start()

    parts[me] = sums[me]
    if last:

        @pl.loop(1, n_dev if spread else n_row)
        def _(step):
            g_copy(step).start()

        g_out[me if spread else row] = g[col if spread else 0]

    @pl.loop(1, n_dev)
    def _(step):
        sum_copy(step).wait()

    spot = col if last else me
    f_out[spot] = f[me] - lse2(parts[...]) / (2 * SCALE)
    amount, where = (n_col, by_col) if last else (n_dev, anyone)

    def f_copy(step):
        return remote(
            f_out.at[spot], f_out.at[spot], f_send.at[step], f_recv.at[step], where(step)
        )

    @pl.loop(1, amount)
    def _(step):
        f_copy(step).start()

    if last:

        @pl.loop(1, n_dev if spread else n_row)
        def _(step):
            g_copy(step).wait()

    @pl.loop(1, amount)
    def _(step):
        f_copy(step).wait()


def exchange(n_row, n_col, spread, last, sums, f, g):
    n_dev = n_row * n_col
    dma = pltpu.SemaphoreType.DMA
    sums, f = (a.reshape(n_dev, -1, 128) for a in (sums, f))
    amount = n_col if last else n_dev
    out = [jax.ShapeDtypeStruct((amount,) + f.shape[1:], f.dtype)]
    scratch = [VMEM(sums.shape, sums.dtype)] + [dma((n_dev,))] * 2 + [dma((amount,))] * 2
    args = [sums, f]
    if last:
        fan = n_dev if spread else n_row
        g = g.reshape(n_col if spread else 1, -1, 128)
        out.append(jax.ShapeDtypeStruct((fan,) + g.shape[1:], g.dtype))
        scratch += [dma((fan,))] * 2
        args.append(g)
    return pl.pallas_call(
        functools.partial(exchange_kernel, n_row, n_col, spread, last),
        out_shape=tuple(out),
        in_specs=[pl.BlockSpec(memory_space=VMEM)] * len(args),
        out_specs=(pl.BlockSpec(memory_space=VMEM),) * len(out),
        scratch_shapes=scratch,
        compiler_params=pltpu.CompilerParams(
            collective_id=2 if last else 1,
            has_side_effects=True,
            vmem_limit_bytes=32 * 1024 * 1024,
        ),
    )(*args)


def on_device(n_row, n_col, source_points, target_points, source_level, target_level, neighbours):
    group = target_points.shape[1] // BLOCK
    share = group // n_row
    spread = share % n_col == 0
    me_row, me_col = lax.axis_index("row"), lax.axis_index("col")
    start, length = me_row * share * BLOCK, share * BLOCK
    source = jnp.concatenate([source_points, source_level[None]], axis=0)
    target = jnp.concatenate(
        [
            lax.dynamic_slice_in_dim(target_points, start, length, 1),
            lax.dynamic_slice_in_dim(target_level, start, length, 0)[None],
        ],
        axis=0,
    )
    if spread:
        target = target.reshape(4, n_col, -1).transpose(1, 0, 2)
        part = share // n_col
        own = (
            jnp.arange(n_col)[:, None] * group
            + me_row * share + me_col * part + jnp.arange(part)[None, :]
        ).reshape(-1)
    else:
        target = target[None]
        own = me_col * group + me_row * share + jnp.arange(share)
    source, lists, target = gather(n_row, n_col, spread, source, neighbours, target)
    lists = lists.reshape(-1, lists.shape[-1])
    f, g = source[:, 3], target[:, 3]
    rows = lists.shape[0]
    cols = own.shape[0]
    capacity = rows * cols
    mask = jnp.any(lists[None] == own[:, None, None], axis=2).reshape(-1)
    order = jnp.arange(capacity)
    place = jnp.sum(jnp.where((order[None, :] <= order[:, None]) & mask[None, :], 1, 0), axis=1)
    count = jnp.max(place)
    slot = jnp.arange(-(-capacity // UNROLL) * UNROLL + 1)
    hit = mask[None, :] & (place[None, :] == slot[:, None] + 1)
    code = order % rows + (order // rows) * 65536
    pick = jnp.sum(jnp.where(hit, code[None, :], 0), axis=1)
    pairs = jnp.where(slot < count, pick, rows + cols * 65536)
    pairs = jnp.where(slot == slot.shape[0] - 1, count, pairs)

    for turn in range(ITERS):
        sums, g = sweep(pairs, source, f, target, g)
        if turn < ITERS - 1:
            (f,) = exchange(n_row, n_col, spread, False, sums, f, None)
    f, g = exchange(n_row, n_col, spread, True, sums, f, g)
    return f.reshape(-1), g.reshape(-1)


def solution(mesh):
    return jax.shard_map(
        functools.partial(on_device, mesh.shape["row"], mesh.shape["col"]),
        mesh=mesh,
        in_specs=(P(None, "row"), P(None, "col"), P("row"), P("col"), P("row", None)),
        out_specs=(P("row"), P("col")),
        check_vma=False,
    )
```

```python
import functools
import math

import jax
import jax.numpy as jnp
from jax import lax
from jax.experimental import pallas as pl
from jax.experimental.pallas import tpu as pltpu
from jax.sharding import PartitionSpec as P

BLOCK = 256
ITERS = 2
EPS = 0.02
SCALE = math.log2(math.e) / EPS
NEG = -1e30
UNROLL = 8
CUT = 4
DEPTH = 48
VMEM = pltpu.VMEM
SMEM = pltpu.SMEM


def pieces(values):
    first = values.astype(jnp.bfloat16).astype(jnp.float32)
    rest = values - first
    second = rest.astype(jnp.bfloat16).astype(jnp.float32)
    return first, second, rest - second


def augmented(points, level, source):
    packed = jnp.concatenate([points, points], axis=0)
    place = lax.broadcasted_iota(jnp.int32, packed.shape, 0)
    squares = jnp.where(place < 3, packed * packed, 0.0)
    norm = jnp.sum(squares, axis=0, keepdims=True)
    level = SCALE * (level - 0.5 * norm)
    if source:
        level_at, one_at, coordinates = 3, 4, SCALE * packed
    else:
        level_at, one_at, coordinates = 4, 3, packed
    rows = jnp.where(
        place < 3,
        coordinates,
        jnp.where(place == level_at, level, jnp.where(place == one_at, 1.0, 0.0)),
    )
    a, b, c = pieces(rows)
    if source:
        return jnp.concatenate([a, a, b, b, a, c], axis=0)
    return jnp.concatenate([a, b, a, b, c, a], axis=0)


def slot_lse(scores):
    depth = scores.shape[0] // CUT
    tops, masses = [], []
    for at in range(CUT):
        tiles = scores[at * depth : (at + 1) * depth].reshape(depth // 8, 8, scores.shape[1])
        top = jnp.max(tiles, axis=0)
        tops.append(top)
        masses.append(jnp.sum(jnp.exp2(tiles - top[None]), axis=0))
    peak = functools.reduce(jnp.maximum, tops)
    return peak, sum(mass * jnp.exp2(top - peak) for top, mass in zip(tops, masses))


def merge(top_ref, mass_ref, at, top, mass):
    old = top_ref[at]
    new = jnp.maximum(old, top)
    top_ref[at] = new
    mass_ref[at] = mass_ref[at] * jnp.exp2(old - new) + mass * jnp.exp2(top - new)


def total(top, mass):
    peak = jnp.max(top, axis=1)
    amount = jnp.sum(mass * jnp.exp2(top - peak[:, None, :]), axis=1)
    return peak + jnp.log2(jnp.maximum(amount, 1e-30))


def sweep_kernel(
    pairs, source, f, target, g, row_out, g_out,
    x_all, xt_all, y_all, yt_all, row_top, row_mass, col_top, col_mass,
):
    rows, cols = f.shape[0], g.shape[0]

    def build(at, ref, level, straight, turned, is_source):
        per = ref.shape[2] // BLOCK
        lanes = pl.ds(pl.multiple_of(at % per * BLOCK, BLOCK), BLOCK)
        block = augmented(ref[at // per, :, lanes], level[at], is_source)
        turned[at] = block.astype(jnp.bfloat16)
        straight[at] = block.T.astype(jnp.bfloat16)

    @pl.loop(0, rows, unroll=4)
    def _(at):
        build(at, source, f, x_all, xt_all, True)

    for at in range(cols):
        build(at, target, g, y_all, yt_all, False)
    x_all[rows] = jnp.zeros_like(x_all[rows])
    xt_all[rows] = jnp.zeros_like(xt_all[rows])
    y_all[cols] = jnp.zeros_like(y_all[cols])
    yt_all[cols] = jnp.zeros_like(yt_all[cols])
    row_top[...] = jnp.full_like(row_top, NEG)
    row_mass[...] = jnp.zeros_like(row_mass)
    col_top[...] = jnp.full_like(col_top, NEG)
    col_mass[...] = jnp.zeros_like(col_mass)

    @pl.loop(0, (pairs[pairs.shape[0] - 1] + UNROLL - 1) // UNROLL)
    def _(turn):
        found = []
        for lane in range(UNROLL):
            pair = pairs[turn * UNROLL + lane]
            row, col = pair & 0xFFFF, pair >> 16
            by_col = jnp.dot(x_all[row], yt_all[col], preferred_element_type=jnp.float32)
            by_row = jnp.dot(y_all[col], xt_all[row], preferred_element_type=jnp.float32)
            found.append((row, col, slot_lse(by_row), slot_lse(by_col)))
        for row, col, of_row, of_col in found:
            merge(row_top, row_mass, row, *of_row)
            merge(col_top, col_mass, col, *of_col)

    row_out[...] = total(row_top[:rows], row_mass[:rows])
    g_out[...] = g[:, 0, :] - total(col_top[:cols], col_mass[:cols]) / (2 * SCALE)


def sweep(pairs, source, f, target, g):
    f, g = f.reshape(-1, 1, BLOCK), g.reshape(-1, 1, BLOCK)
    rows, cols = f.shape[0], g.shape[0]
    bf16, f32 = jnp.bfloat16, jnp.float32
    return pl.pallas_call(
        sweep_kernel,
        out_shape=(
            jax.ShapeDtypeStruct((rows, BLOCK), f32),
            jax.ShapeDtypeStruct((cols, BLOCK), f32),
        ),
        in_specs=[pl.BlockSpec(memory_space=SMEM)] + [pl.BlockSpec(memory_space=VMEM)] * 4,
        out_specs=(pl.BlockSpec(memory_space=VMEM),) * 2,
        scratch_shapes=[
            VMEM((rows + 1, BLOCK, DEPTH), bf16),
            VMEM((rows + 1, DEPTH, BLOCK), bf16),
            VMEM((cols + 1, BLOCK, DEPTH), bf16),
            VMEM((cols + 1, DEPTH, BLOCK), bf16),
            VMEM((rows + 1, 8, BLOCK), f32),
            VMEM((rows + 1, 8, BLOCK), f32),
            VMEM((cols + 1, 8, BLOCK), f32),
            VMEM((cols + 1, 8, BLOCK), f32),
        ],
        compiler_params=pltpu.CompilerParams(vmem_limit_bytes=48 * 1024 * 1024),
    )(pairs, source, f, target, g)


def lse2(parts):
    peak = jnp.max(parts, axis=0)
    return peak + jnp.log2(jnp.sum(jnp.exp2(parts - peak[None]), axis=0))


def wrap(value, size):
    return jnp.where(value >= size, value - size, value)


def settle(ref, amount, semaphore):
    chunks = ref.at[pl.ds(0, amount)]
    pltpu.make_async_copy(chunks, chunks, semaphore).wait()


def each_peer(n_row, n_col, visit):
    for col_step in range(1, n_col):
        visit(0, col_step)

    @pl.loop(1, n_row)
    def _(row_step):
        for col_step in range(n_col):
            visit(row_step, col_step)


def meet(peers):
    barrier = pltpu.get_barrier_semaphore()
    for amount, where in peers:

        @pl.loop(1, amount)
        def _(step):
            pl.semaphore_signal(
                barrier, inc=1, device_id=where(step), device_id_type=pl.DeviceIdType.MESH
            )

    pl.semaphore_wait(barrier, sum(amount - 1 for amount, _ in peers))


def remote(src, dst, send, recv, where):
    return pltpu.make_async_remote_copy(
        src_ref=src, dst_ref=dst, send_sem=send, recv_sem=recv,
        device_id=where, device_id_type=pl.DeviceIdType.MESH,
    )


def gather_kernel(
    n_row, n_col, spread, source, lists, target, source_out, lists_out, target_out,
    source_send, source_recv, lists_send, lists_recv, target_send, target_recv,
):
    row, col = lax.axis_index("row"), lax.axis_index("col")

    def by_row(step):
        return (lax.rem(row + step, n_row), col)

    def by_col(step):
        return (row, lax.rem(col + step, n_col))

    meet([(n_row, by_row)] + ([(n_col, by_col)] if spread else []))

    def copies(step):
        to = by_row(step)
        return (
            remote(source, source_out.at[row], source_send.at[step], source_recv.at[step], to),
            remote(lists, lists_out.at[row], lists_send.at[step], lists_recv.at[step], to),
        )

    def target_copy(step):
        to = by_col(step)
        return remote(
            target.at[to[1]], target_out.at[col], target_send.at[step], target_recv.at[step], to
        )

    @pl.loop(1, n_row)
    def _(step):
        for copy in copies(step):
            copy.start()

    if spread:

        @pl.loop(1, n_col)
        def _(step):
            target_copy(step).start()

        target_out[col] = target[col]

        @pl.loop(1, n_col)
        def _(step):
            target_copy(step).wait()
    else:
        target_out[...] = target[...]

    source_out[row] = source[...]
    lists_out[row] = lists[...]

    @pl.loop(1, n_row)
    def _(step):
        for copy in copies(step):
            copy.wait()


def gather(n_row, n_col, spread, source, lists, target):
    dma = pltpu.SemaphoreType.DMA
    return pl.pallas_call(
        functools.partial(gather_kernel, n_row, n_col, spread),
        out_shape=(
            jax.ShapeDtypeStruct((n_row,) + source.shape, source.dtype),
            jax.ShapeDtypeStruct((n_row,) + lists.shape, lists.dtype),
            jax.ShapeDtypeStruct(target.shape, target.dtype),
        ),
        in_specs=[pl.BlockSpec(memory_space=VMEM)] * 3,
        out_specs=(pl.BlockSpec(memory_space=VMEM),) * 3,
        scratch_shapes=[dma((n_row,))] * 4 + [dma((n_col,))] * 2,
        compiler_params=pltpu.CompilerParams(
            collective_id=0, has_side_effects=True, vmem_limit_bytes=32 * 1024 * 1024
        ),
    )(source, lists, target)


def exchange_kernel(n_row, n_col, spread, last, *refs):
    if last:
        (
            sums, f, g, f_out, g_out,
            parts, send, recv, f_send, f_recv, g_send, g_recv,
        ) = refs
    else:
        sums, f, f_out, parts, send, recv, f_send, f_recv = refs
    n_dev = n_row * n_col
    row, col = lax.axis_index("row"), lax.axis_index("col")
    me = row * n_col + col

    def peer(row_step, col_step):
        return wrap(row + row_step, n_row), wrap(col + col_step, n_col)

    def greet(row_step, col_step):
        pl.semaphore_signal(
            barrier, inc=1, device_id=peer(row_step, col_step),
            device_id_type=pl.DeviceIdType.MESH,
        )

    def send_sum(row_step, col_step):
        to = peer(row_step, col_step)
        remote(sums.at[to[0] * n_col + to[1]], parts.at[me], send, recv, to).start()

    def send_g(row_step, col_step):
        to = peer(row_step, col_step)
        remote(
            g.at[to[1] if spread else 0], g_out.at[me if spread else row], g_send, g_recv, to
        ).start()

    def send_f(row_step, col_step):
        remote(
            f_out.at[spot], f_out.at[spot], f_send, f_recv, peer(row_step, col_step)
        ).start()

    barrier = pltpu.get_barrier_semaphore()
    each_peer(n_row, n_col, greet)
    pl.semaphore_wait(barrier, n_dev - 1)
    each_peer(n_row, n_col, send_sum)
    parts[me] = sums[me]
    if last:
        each_peer(n_row, n_col if spread else 1, send_g)
        g_out[me if spread else row] = g[col if spread else 0]
    settle(parts, n_dev - 1, recv)
    spot = col if last else me
    f_out[spot] = f[me] - lse2(parts[...]) / (2 * SCALE)
    each_peer(1 if last else n_row, n_col, send_f)
    settle(parts, n_dev - 1, send)
    if last:
        others = (n_dev if spread else n_row) - 1
        settle(g_out, others, g_send)
        settle(g_out, others, g_recv)
    others = (n_col if last else n_dev) - 1
    settle(f_out, others, f_send)
    settle(f_out, others, f_recv)


def exchange(n_row, n_col, spread, last, sums, f, g):
    n_dev = n_row * n_col
    dma = pltpu.SemaphoreType.DMA
    sums, f = (a.reshape(n_dev, -1, 128) for a in (sums, f))
    amount = n_col if last else n_dev
    out = [jax.ShapeDtypeStruct((amount,) + f.shape[1:], f.dtype)]
    scratch = [VMEM(sums.shape, sums.dtype)] + [dma] * 4
    args = [sums, f]
    if last:
        fan = n_dev if spread else n_row
        g = g.reshape(n_col if spread else 1, -1, 128)
        out.append(jax.ShapeDtypeStruct((fan,) + g.shape[1:], g.dtype))
        scratch += [dma] * 2
        args.append(g)
    return pl.pallas_call(
        functools.partial(exchange_kernel, n_row, n_col, spread, last),
        out_shape=tuple(out),
        in_specs=[pl.BlockSpec(memory_space=VMEM)] * len(args),
        out_specs=(pl.BlockSpec(memory_space=VMEM),) * len(out),
        scratch_shapes=scratch,
        compiler_params=pltpu.CompilerParams(
            collective_id=2 if last else 1,
            has_side_effects=True,
            vmem_limit_bytes=32 * 1024 * 1024,
        ),
    )(*args)


def on_device(n_row, n_col, source_points, target_points, source_level, target_level, neighbours):
    group = target_points.shape[1] // BLOCK
    share = group // n_row
    spread = share % n_col == 0
    me_row, me_col = lax.axis_index("row"), lax.axis_index("col")
    start, length = me_row * share * BLOCK, share * BLOCK
    source = jnp.concatenate([source_points, source_level[None]], axis=0)
    target = jnp.concatenate(
        [
            lax.dynamic_slice_in_dim(target_points, start, length, 1),
            lax.dynamic_slice_in_dim(target_level, start, length, 0)[None],
        ],
        axis=0,
    )
    if spread:
        target = target.reshape(4, n_col, -1).transpose(1, 0, 2)
        part = share // n_col
        own = (
            jnp.arange(n_col)[:, None] * group
            + me_row * share + me_col * part + jnp.arange(part)[None, :]
        ).reshape(-1)
    else:
        target = target[None]
        own = me_col * group + me_row * share + jnp.arange(share)
    source, lists, target = gather(n_row, n_col, spread, source, neighbours, target)
    lists = lists.reshape(-1, lists.shape[-1])
    f, g = source[:, 3], target[:, 3]
    rows = lists.shape[0]
    cols = own.shape[0]
    capacity = rows * cols
    mask = jnp.any(lists[None] == own[:, None, None], axis=2).reshape(-1)
    order = jnp.arange(capacity)
    place = jnp.sum(jnp.where((order[None, :] <= order[:, None]) & mask[None, :], 1, 0), axis=1)
    count = jnp.max(place)
    slot = jnp.arange(-(-capacity // UNROLL) * UNROLL + 1)
    hit = mask[None, :] & (place[None, :] == slot[:, None] + 1)
    code = order % rows + (order // rows) * 65536
    pick = jnp.sum(jnp.where(hit, code[None, :], 0), axis=1)
    pairs = jnp.where(slot < count, pick, rows + cols * 65536)
    pairs = jnp.where(slot == slot.shape[0] - 1, count, pairs)

    for turn in range(ITERS):
        sums, g = sweep(pairs, source, f, target, g)
        if turn < ITERS - 1:
            (f,) = exchange(n_row, n_col, spread, False, sums, f, None)
    f, g = exchange(n_row, n_col, spread, True, sums, f, g)
    return f.reshape(-1), g.reshape(-1)


def solution(mesh):
    return jax.shard_map(
        functools.partial(on_device, mesh.shape["row"], mesh.shape["col"]),
        mesh=mesh,
        in_specs=(P(None, "row"), P(None, "col"), P("row"), P("col"), P("row", None)),
        out_specs=(P("row"), P("col")),
        check_vma=False,
    )
```

```python
import functools
import math

import jax
import jax.numpy as jnp
from jax import lax
from jax.experimental import pallas as pl
from jax.experimental.pallas import tpu as pltpu
from jax.sharding import PartitionSpec as P

BLOCK = 256
ITERS = 2
EPS = 0.02
SCALE = math.log2(math.e) / EPS
NEG = -1e30
UNROLL = 8
CUT = 4
DEPTH = 48
VMEM = pltpu.VMEM
SMEM = pltpu.SMEM


def pieces(values):
    first = values.astype(jnp.bfloat16).astype(jnp.float32)
    rest = values - first
    second = rest.astype(jnp.bfloat16).astype(jnp.float32)
    return first, second, rest - second


def augmented(points, level, source):
    packed = jnp.concatenate([points, points], axis=0)
    place = lax.broadcasted_iota(jnp.int32, packed.shape, 0)
    squares = jnp.where(place < 3, packed * packed, 0.0)
    norm = jnp.sum(squares, axis=0, keepdims=True)
    level = SCALE * (level - 0.5 * norm)
    if source:
        level_at, one_at, coordinates = 3, 4, SCALE * packed
    else:
        level_at, one_at, coordinates = 4, 3, packed
    rows = jnp.where(
        place < 3,
        coordinates,
        jnp.where(place == level_at, level, jnp.where(place == one_at, 1.0, 0.0)),
    )
    a, b, c = pieces(rows)
    if source:
        return jnp.concatenate([a, a, b, b, a, c], axis=0)
    return jnp.concatenate([a, b, a, b, c, a], axis=0)


def slot_lse(scores):
    depth = scores.shape[0] // CUT
    tops, masses = [], []
    for at in range(CUT):
        tiles = scores[at * depth : (at + 1) * depth].reshape(depth // 8, 8, scores.shape[1])
        top = jnp.max(tiles, axis=0)
        tops.append(top)
        masses.append(jnp.sum(jnp.exp2(tiles - top[None]), axis=0))
    peak = functools.reduce(jnp.maximum, tops)
    return peak, sum(mass * jnp.exp2(top - peak) for top, mass in zip(tops, masses))


def merge(top_ref, mass_ref, at, top, mass):
    old = top_ref[at]
    new = jnp.maximum(old, top)
    top_ref[at] = new
    mass_ref[at] = mass_ref[at] * jnp.exp2(old - new) + mass * jnp.exp2(top - new)


def total(top, mass):
    peak = jnp.max(top, axis=1)
    amount = jnp.sum(mass * jnp.exp2(top - peak[:, None, :]), axis=1)
    return peak + jnp.log2(jnp.maximum(amount, 1e-30))


def sweep_kernel(
    pairs, source, f, target, g, row_out, g_out,
    x_all, xt_all, y_all, yt_all, row_top, row_mass, col_top, col_mass,
):
    rows, cols = f.shape[0], g.shape[0]

    def build(at, ref, level, straight, turned, is_source):
        per = ref.shape[2] // BLOCK
        lanes = pl.ds(pl.multiple_of(at % per * BLOCK, BLOCK), BLOCK)
        block = augmented(ref[at // per, :, lanes], level[at], is_source)
        turned[at] = block.astype(jnp.bfloat16)
        straight[at] = block.T.astype(jnp.bfloat16)

    @pl.loop(0, rows, unroll=4)
    def _(at):
        build(at, source, f, x_all, xt_all, True)

    for at in range(cols):
        build(at, target, g, y_all, yt_all, False)
    x_all[rows] = jnp.zeros_like(x_all[rows])
    xt_all[rows] = jnp.zeros_like(xt_all[rows])
    y_all[cols] = jnp.zeros_like(y_all[cols])
    yt_all[cols] = jnp.zeros_like(yt_all[cols])
    row_top[...] = jnp.full_like(row_top, NEG)
    row_mass[...] = jnp.zeros_like(row_mass)
    col_top[...] = jnp.full_like(col_top, NEG)
    col_mass[...] = jnp.zeros_like(col_mass)

    @pl.loop(0, (pairs[pairs.shape[0] - 1] + UNROLL - 1) // UNROLL)
    def _(turn):
        found = []
        for lane in range(UNROLL):
            pair = pairs[turn * UNROLL + lane]
            row, col = pair & 0xFFFF, (pair >> 16) - 1
            by_col = jnp.dot(x_all[row], yt_all[col], preferred_element_type=jnp.float32)
            by_row = jnp.dot(y_all[col], xt_all[row], preferred_element_type=jnp.float32)
            found.append((row, col, slot_lse(by_row), slot_lse(by_col)))
        for row, col, of_row, of_col in found:
            merge(row_top, row_mass, row, *of_row)
            merge(col_top, col_mass, col, *of_col)

    row_out[...] = total(row_top[:rows], row_mass[:rows])
    g_out[...] = g[:, 0, :] - total(col_top[:cols], col_mass[:cols]) / (2 * SCALE)


def sweep(pairs, source, f, target, g):
    f, g = f.reshape(-1, 1, BLOCK), g.reshape(-1, 1, BLOCK)
    rows, cols = f.shape[0], g.shape[0]
    bf16, f32 = jnp.bfloat16, jnp.float32
    return pl.pallas_call(
        sweep_kernel,
        out_shape=(
            jax.ShapeDtypeStruct((rows, BLOCK), f32),
            jax.ShapeDtypeStruct((cols, BLOCK), f32),
        ),
        in_specs=[pl.BlockSpec(memory_space=SMEM)] + [pl.BlockSpec(memory_space=VMEM)] * 4,
        out_specs=(pl.BlockSpec(memory_space=VMEM),) * 2,
        scratch_shapes=[
            VMEM((rows + 1, BLOCK, DEPTH), bf16),
            VMEM((rows + 1, DEPTH, BLOCK), bf16),
            VMEM((cols + 1, BLOCK, DEPTH), bf16),
            VMEM((cols + 1, DEPTH, BLOCK), bf16),
            VMEM((rows + 1, 8, BLOCK), f32),
            VMEM((rows + 1, 8, BLOCK), f32),
            VMEM((cols + 1, 8, BLOCK), f32),
            VMEM((cols + 1, 8, BLOCK), f32),
        ],
        compiler_params=pltpu.CompilerParams(vmem_limit_bytes=48 * 1024 * 1024),
    )(pairs, source, f, target, g)


def lse2(parts):
    peak = jnp.max(parts, axis=0)
    return peak + jnp.log2(jnp.sum(jnp.exp2(parts - peak[None]), axis=0))


def wrap(value, size):
    return jnp.where(value >= size, value - size, value)


def settle(ref, amount, semaphore):
    chunks = ref.at[pl.ds(0, amount)]
    pltpu.make_async_copy(chunks, chunks, semaphore).wait()


def each_peer(n_row, n_col, visit):
    for col_step in range(1, n_col):
        visit(0, col_step)

    @pl.loop(1, n_row)
    def _(row_step):
        for col_step in range(n_col):
            visit(row_step, col_step)


def meet(peers):
    barrier = pltpu.get_barrier_semaphore()
    for amount, where in peers:

        @pl.loop(1, amount)
        def _(step):
            pl.semaphore_signal(
                barrier, inc=1, device_id=where(step), device_id_type=pl.DeviceIdType.MESH
            )

    pl.semaphore_wait(barrier, sum(amount - 1 for amount, _ in peers))


def remote(src, dst, send, recv, where):
    return pltpu.make_async_remote_copy(
        src_ref=src, dst_ref=dst, send_sem=send, recv_sem=recv,
        device_id=where, device_id_type=pl.DeviceIdType.MESH,
    )


def gather_kernel(
    n_row, n_col, spread, source, lists, target, source_out, lists_out, target_out,
    source_send, source_recv, lists_send, lists_recv, target_send, target_recv,
):
    row, col = lax.axis_index("row"), lax.axis_index("col")

    def by_row(step):
        return (lax.rem(row + step, n_row), col)

    def by_col(step):
        return (row, lax.rem(col + step, n_col))

    meet([(n_row, by_row)] + ([(n_col, by_col)] if spread else []))

    def copies(step):
        to = by_row(step)
        return (
            remote(source, source_out.at[row], source_send.at[step], source_recv.at[step], to),
            remote(lists, lists_out.at[row], lists_send.at[step], lists_recv.at[step], to),
        )

    def target_copy(step):
        to = by_col(step)
        return remote(
            target.at[to[1]], target_out.at[col], target_send.at[step], target_recv.at[step], to
        )

    @pl.loop(1, n_row)
    def _(step):
        for copy in copies(step):
            copy.start()

    if spread:

        @pl.loop(1, n_col)
        def _(step):
            target_copy(step).start()

        target_out[col] = target[col]

        @pl.loop(1, n_col)
        def _(step):
            target_copy(step).wait()
    else:
        target_out[...] = target[...]

    source_out[row] = source[...]
    lists_out[row] = lists[...]

    @pl.loop(1, n_row)
    def _(step):
        for copy in copies(step):
            copy.wait()


def gather(n_row, n_col, spread, source, lists, target):
    dma = pltpu.SemaphoreType.DMA
    return pl.pallas_call(
        functools.partial(gather_kernel, n_row, n_col, spread),
        out_shape=(
            jax.ShapeDtypeStruct((n_row,) + source.shape, source.dtype),
            jax.ShapeDtypeStruct((n_row,) + lists.shape, lists.dtype),
            jax.ShapeDtypeStruct(target.shape, target.dtype),
        ),
        in_specs=[pl.BlockSpec(memory_space=VMEM)] * 3,
        out_specs=(pl.BlockSpec(memory_space=VMEM),) * 3,
        scratch_shapes=[dma((n_row,))] * 4 + [dma((n_col,))] * 2,
        compiler_params=pltpu.CompilerParams(
            collective_id=0, has_side_effects=True, vmem_limit_bytes=32 * 1024 * 1024
        ),
    )(source, lists, target)


def exchange_kernel(n_row, n_col, spread, last, *refs):
    if last:
        (
            sums, f, g, f_out, g_out,
            parts, send, recv, f_send, f_recv, g_send, g_recv,
        ) = refs
    else:
        sums, f, f_out, parts, send, recv, f_send, f_recv = refs
    n_dev = n_row * n_col
    row, col = lax.axis_index("row"), lax.axis_index("col")
    me = row * n_col + col

    def peer(row_step, col_step):
        return wrap(row + row_step, n_row), wrap(col + col_step, n_col)

    def greet(row_step, col_step):
        pl.semaphore_signal(
            barrier, inc=1, device_id=peer(row_step, col_step),
            device_id_type=pl.DeviceIdType.MESH,
        )

    def send_sum(row_step, col_step):
        to = peer(row_step, col_step)
        remote(sums.at[to[0] * n_col + to[1]], parts.at[me], send, recv, to).start()

    def send_g(row_step, col_step):
        to = peer(row_step, col_step)
        remote(
            g.at[to[1] if spread else 0], g_out.at[me if spread else row], g_send, g_recv, to
        ).start()

    def send_f(row_step, col_step):
        remote(
            f_out.at[spot], f_out.at[spot], f_send, f_recv, peer(row_step, col_step)
        ).start()

    barrier = pltpu.get_barrier_semaphore()
    each_peer(n_row, n_col, greet)
    pl.semaphore_wait(barrier, n_dev - 1)
    each_peer(n_row, n_col, send_sum)
    parts[me] = sums[me]
    if last:
        each_peer(n_row, n_col if spread else 1, send_g)
        g_out[me if spread else row] = g[col if spread else 0]
    settle(parts, n_dev - 1, recv)
    spot = col if last else me
    f_out[spot] = f[me] - lse2(parts[...]) / (2 * SCALE)
    each_peer(1 if last else n_row, n_col, send_f)
    settle(parts, n_dev - 1, send)
    if last:
        others = (n_dev if spread else n_row) - 1
        settle(g_out, others, g_send)
        settle(g_out, others, g_recv)
    others = (n_col if last else n_dev) - 1
    settle(f_out, others, f_send)
    settle(f_out, others, f_recv)


def exchange(n_row, n_col, spread, last, sums, f, g):
    n_dev = n_row * n_col
    dma = pltpu.SemaphoreType.DMA
    sums, f = (a.reshape(n_dev, -1, 128) for a in (sums, f))
    amount = n_col if last else n_dev
    out = [jax.ShapeDtypeStruct((amount,) + f.shape[1:], f.dtype)]
    scratch = [VMEM(sums.shape, sums.dtype)] + [dma] * 4
    args = [sums, f]
    if last:
        fan = n_dev if spread else n_row
        g = g.reshape(n_col if spread else 1, -1, 128)
        out.append(jax.ShapeDtypeStruct((fan,) + g.shape[1:], g.dtype))
        scratch += [dma] * 2
        args.append(g)
    return pl.pallas_call(
        functools.partial(exchange_kernel, n_row, n_col, spread, last),
        out_shape=tuple(out),
        in_specs=[pl.BlockSpec(memory_space=VMEM)] * len(args),
        out_specs=(pl.BlockSpec(memory_space=VMEM),) * len(out),
        scratch_shapes=scratch,
        compiler_params=pltpu.CompilerParams(
            collective_id=2 if last else 1,
            has_side_effects=True,
            vmem_limit_bytes=32 * 1024 * 1024,
        ),
    )(*args)


def on_device(n_row, n_col, source_points, target_points, source_level, target_level, neighbours):
    group = target_points.shape[1] // BLOCK
    share = group // n_row
    spread = share % n_col == 0
    me_row, me_col = lax.axis_index("row"), lax.axis_index("col")
    start, length = me_row * share * BLOCK, share * BLOCK
    source = jnp.concatenate([source_points, source_level[None]], axis=0)
    target = jnp.concatenate(
        [
            lax.dynamic_slice_in_dim(target_points, start, length, 1),
            lax.dynamic_slice_in_dim(target_level, start, length, 0)[None],
        ],
        axis=0,
    )
    if spread:
        target = target.reshape(4, n_col, -1).transpose(1, 0, 2)
        part = share // n_col
        own = (
            jnp.arange(n_col)[:, None] * group
            + me_row * share + me_col * part + jnp.arange(part)[None, :]
        ).reshape(-1)
    else:
        target = target[None]
        own = me_col * group + me_row * share + jnp.arange(share)
    source, lists, target = gather(n_row, n_col, spread, source, neighbours, target)
    lists = lists.reshape(-1, lists.shape[-1])
    f, g = source[:, 3], target[:, 3]
    rows = lists.shape[0]
    cols = own.shape[0]
    capacity = rows * cols
    mask = jnp.any(lists[None] == own[:, None, None], axis=2).reshape(-1)
    order = jnp.arange(capacity)
    place = jnp.sum(jnp.where((order[None, :] <= order[:, None]) & mask[None, :], 1, 0), axis=1)
    slot = jnp.arange(-(-capacity // UNROLL) * UNROLL + 1)[:, None]
    final = slot == slot.shape[0] - 1
    hit = mask[None, :] & ((place[None, :] == slot + 1) | final)
    code = order % rows + (order // rows + 1) * 65536
    pick = jnp.sum(jnp.where(hit, jnp.where(final, 1, code[None, :]), 0), axis=1)
    pairs = jnp.where(pick == 0, rows + (cols + 1) * 65536, pick)

    for turn in range(ITERS):
        sums, g = sweep(pairs, source, f, target, g)
        if turn < ITERS - 1:
            (f,) = exchange(n_row, n_col, spread, False, sums, f, None)
    f, g = exchange(n_row, n_col, spread, True, sums, f, g)
    return f.reshape(-1), g.reshape(-1)


def solution(mesh):
    return jax.shard_map(
        functools.partial(on_device, mesh.shape["row"], mesh.shape["col"]),
        mesh=mesh,
        in_specs=(P(None, "row"), P(None, "col"), P("row"), P("col"), P("row", None)),
        out_specs=(P("row"), P("col")),
        check_vma=False,
    )
```

```python
import functools
import math

import jax
import jax.numpy as jnp
from jax import lax
from jax.experimental import pallas as pl
from jax.experimental.pallas import tpu as pltpu
from jax.sharding import PartitionSpec as P

BLOCK = 256
ITERS = 2
EPS = 0.02
SCALE = math.log2(math.e) / EPS
NEG = -1e30
UNROLL = 8
CUT = 4
DEPTH = 48
VMEM = pltpu.VMEM
SMEM = pltpu.SMEM


def pieces(values):
    first = values.astype(jnp.bfloat16).astype(jnp.float32)
    rest = values - first
    second = rest.astype(jnp.bfloat16).astype(jnp.float32)
    return first, second, rest - second


def augmented(points, level, source):
    packed = jnp.concatenate([points, points], axis=0)
    place = lax.broadcasted_iota(jnp.int32, packed.shape, 0)
    squares = jnp.where(place < 3, packed * packed, 0.0)
    norm = jnp.sum(squares, axis=0, keepdims=True)
    level = SCALE * (level - 0.5 * norm)
    if source:
        level_at, one_at, coordinates = 3, 4, SCALE * packed
    else:
        level_at, one_at, coordinates = 4, 3, packed
    rows = jnp.where(
        place < 3,
        coordinates,
        jnp.where(place == level_at, level, jnp.where(place == one_at, 1.0, 0.0)),
    )
    a, b, c = pieces(rows)
    if source:
        return jnp.concatenate([a, a, b, b, a, c], axis=0)
    return jnp.concatenate([a, b, a, b, c, a], axis=0)


def slot_lse(scores):
    depth = scores.shape[0] // CUT
    tops, masses = [], []
    for at in range(CUT):
        tiles = scores[at * depth : (at + 1) * depth].reshape(depth // 8, 8, scores.shape[1])
        top = jnp.max(tiles, axis=0)
        tops.append(top)
        masses.append(jnp.sum(jnp.exp2(tiles - top[None]), axis=0))
    peak = functools.reduce(jnp.maximum, tops)
    return peak, sum(mass * jnp.exp2(top - peak) for top, mass in zip(tops, masses))


def merge(top_ref, mass_ref, at, top, mass):
    old = top_ref[at]
    new = jnp.maximum(old, top)
    top_ref[at] = new
    mass_ref[at] = mass_ref[at] * jnp.exp2(old - new) + mass * jnp.exp2(top - new)


def total(top, mass):
    peak = jnp.max(top, axis=1)
    amount = jnp.sum(mass * jnp.exp2(top - peak[:, None, :]), axis=1)
    return peak + jnp.log2(jnp.maximum(amount, 1e-30))


def sweep_kernel(
    pairs, source, f, target, g, row_out, g_out,
    x_all, xt_all, y_all, yt_all, row_top, row_mass, col_top, col_mass,
):
    rows, cols = f.shape[0], g.shape[0]

    def build(at, ref, level, straight, turned, is_source):
        per = ref.shape[2] // BLOCK
        lanes = pl.ds(pl.multiple_of(at % per * BLOCK, BLOCK), BLOCK)
        block = augmented(ref[at // per, :, lanes], level[at], is_source)
        turned[at] = block.astype(jnp.bfloat16)
        straight[at] = block.T.astype(jnp.bfloat16)

    @pl.loop(0, rows, unroll=4)
    def _(at):
        build(at, source, f, x_all, xt_all, True)

    for at in range(cols):
        build(at, target, g, y_all, yt_all, False)
    x_all[rows] = jnp.zeros_like(x_all[rows])
    xt_all[rows] = jnp.zeros_like(xt_all[rows])
    y_all[cols] = jnp.zeros_like(y_all[cols])
    yt_all[cols] = jnp.zeros_like(yt_all[cols])
    row_top[...] = jnp.full_like(row_top, NEG)
    row_mass[...] = jnp.zeros_like(row_mass)
    col_top[...] = jnp.full_like(col_top, NEG)
    col_mass[...] = jnp.zeros_like(col_mass)

    @pl.loop(0, (pairs[pairs.shape[0] - 1] + UNROLL - 1) // UNROLL)
    def _(turn):
        found = []
        for lane in range(UNROLL):
            pair = pairs[turn * UNROLL + lane]
            row, col = pair & 0xFFFF, pair >> 16
            by_col = jnp.dot(x_all[row], yt_all[col], preferred_element_type=jnp.float32)
            by_row = jnp.dot(y_all[col], xt_all[row], preferred_element_type=jnp.float32)
            found.append((row, col, slot_lse(by_row), slot_lse(by_col)))
        for row, col, of_row, of_col in found:
            merge(row_top, row_mass, row, *of_row)
            merge(col_top, col_mass, col, *of_col)

    row_out[...] = total(row_top[:rows], row_mass[:rows])
    g_out[...] = g[:, 0, :] - total(col_top[:cols], col_mass[:cols]) / (2 * SCALE)


def sweep(pairs, source, f, target, g):
    f, g = f.reshape(-1, 1, BLOCK), g.reshape(-1, 1, BLOCK)
    rows, cols = f.shape[0], g.shape[0]
    bf16, f32 = jnp.bfloat16, jnp.float32
    return pl.pallas_call(
        sweep_kernel,
        out_shape=(
            jax.ShapeDtypeStruct((rows, BLOCK), f32),
            jax.ShapeDtypeStruct((cols, BLOCK), f32),
        ),
        in_specs=[pl.BlockSpec(memory_space=SMEM)] + [pl.BlockSpec(memory_space=VMEM)] * 4,
        out_specs=(pl.BlockSpec(memory_space=VMEM),) * 2,
        scratch_shapes=[
            VMEM((rows + 1, BLOCK, DEPTH), bf16),
            VMEM((rows + 1, DEPTH, BLOCK), bf16),
            VMEM((cols + 1, BLOCK, DEPTH), bf16),
            VMEM((cols + 1, DEPTH, BLOCK), bf16),
            VMEM((rows + 1, 8, BLOCK), f32),
            VMEM((rows + 1, 8, BLOCK), f32),
            VMEM((cols + 1, 8, BLOCK), f32),
            VMEM((cols + 1, 8, BLOCK), f32),
        ],
        compiler_params=pltpu.CompilerParams(vmem_limit_bytes=48 * 1024 * 1024),
    )(pairs, source, f, target, g)


def lse2(parts):
    peak = jnp.max(parts, axis=0)
    return peak + jnp.log2(jnp.sum(jnp.exp2(parts - peak[None]), axis=0))


def wrap(value, size):
    return jnp.where(value >= size, value - size, value)


def settle(ref, amount, semaphore):
    chunks = ref.at[pl.ds(0, amount)]
    pltpu.make_async_copy(chunks, chunks, semaphore).wait()


def each_peer(n_row, n_col, visit):
    for col_step in range(1, n_col):
        visit(0, col_step)

    @pl.loop(1, n_row)
    def _(row_step):
        for col_step in range(n_col):
            visit(row_step, col_step)


def meet(peers):
    barrier = pltpu.get_barrier_semaphore()
    for amount, where in peers:

        @pl.loop(1, amount)
        def _(step):
            pl.semaphore_signal(
                barrier, inc=1, device_id=where(step), device_id_type=pl.DeviceIdType.MESH
            )

    pl.semaphore_wait(barrier, sum(amount - 1 for amount, _ in peers))


def remote(src, dst, send, recv, where):
    return pltpu.make_async_remote_copy(
        src_ref=src, dst_ref=dst, send_sem=send, recv_sem=recv,
        device_id=where, device_id_type=pl.DeviceIdType.MESH,
    )


def gather_kernel(
    n_row, n_col, spread, source, lists, target, source_out, lists_out, target_out,
    source_send, source_recv, lists_send, lists_recv, target_send, target_recv,
    pair_send, pair_recv,
):
    row, col = lax.axis_index("row"), lax.axis_index("col")

    def by_row(step):
        return (lax.rem(row + step, n_row), col)

    def by_col(step):
        return (row, lax.rem(col + step, n_col))

    def sibling(step):
        return (row, col + 1 - 2 * lax.rem(col, 2))

    half = source.shape[1] // 2
    lanes = pl.ds(pl.multiple_of(lax.rem(col, 2) * half, 128), half)
    meet([(n_row, by_row), (n_col, by_col) if spread else (2, sibling)])

    def copies(step):
        to = by_row(step)
        return (
            remote(source.at[:, lanes], source_out.at[row, :, lanes], source_send.at[step], source_recv.at[step], to),
            remote(lists, lists_out.at[row], lists_send.at[step], lists_recv.at[step], to),
        )

    def target_copy(step):
        to = by_col(step)
        return remote(
            target.at[to[1]], target_out.at[col], target_send.at[step], target_recv.at[step], to
        )

    @pl.loop(1, n_row)
    def _(step):
        for copy in copies(step):
            copy.start()

    if spread:

        @pl.loop(1, n_col)
        def _(step):
            target_copy(step).start()

        target_out[col] = target[col]

        @pl.loop(1, n_col)
        def _(step):
            target_copy(step).wait()
    else:
        target_out[...] = target[...]

    source_out[row, :, lanes] = source[:, lanes]
    lists_out[row] = lists[...]

    @pl.loop(1, n_row)
    def _(step):
        for copy in copies(step):
            copy.wait()

    mine = source_out.at[:, :, lanes]
    pair = remote(mine, mine, pair_send, pair_recv, sibling(1))
    pair.start()
    pair.wait()


def gather(n_row, n_col, spread, source, lists, target):
    dma = pltpu.SemaphoreType.DMA
    return pl.pallas_call(
        functools.partial(gather_kernel, n_row, n_col, spread),
        out_shape=(
            jax.ShapeDtypeStruct((n_row,) + source.shape, source.dtype),
            jax.ShapeDtypeStruct((n_row,) + lists.shape, lists.dtype),
            jax.ShapeDtypeStruct(target.shape, target.dtype),
        ),
        in_specs=[pl.BlockSpec(memory_space=VMEM)] * 3,
        out_specs=(pl.BlockSpec(memory_space=VMEM),) * 3,
        scratch_shapes=[dma((n_row,))] * 4 + [dma((n_col,))] * 2 + [dma] * 2,
        compiler_params=pltpu.CompilerParams(
            collective_id=0, has_side_effects=True, vmem_limit_bytes=32 * 1024 * 1024
        ),
    )(source, lists, target)


def exchange_kernel(n_row, n_col, spread, last, *refs):
    if last:
        (
            sums, f, g, f_out, g_out,
            parts, send, recv, f_send, f_recv, g_send, g_recv,
        ) = refs
    else:
        sums, f, f_out, parts, send, recv, f_send, f_recv = refs
    n_dev = n_row * n_col
    row, col = lax.axis_index("row"), lax.axis_index("col")
    me = row * n_col + col

    def peer(row_step, col_step):
        return wrap(row + row_step, n_row), wrap(col + col_step, n_col)

    def greet(row_step, col_step):
        pl.semaphore_signal(
            barrier, inc=1, device_id=peer(row_step, col_step),
            device_id_type=pl.DeviceIdType.MESH,
        )

    def send_sum(row_step, col_step):
        to = peer(row_step, col_step)
        remote(sums.at[to[0] * n_col + to[1]], parts.at[me], send, recv, to).start()

    def send_g(row_step, col_step):
        to = peer(row_step, col_step)
        remote(
            g.at[to[1] if spread else 0], g_out.at[me if spread else row], g_send, g_recv, to
        ).start()

    def send_f(row_step, col_step):
        remote(
            f_out.at[spot], f_out.at[spot], f_send, f_recv, peer(row_step, col_step)
        ).start()

    barrier = pltpu.get_barrier_semaphore()
    each_peer(n_row, n_col, greet)
    pl.semaphore_wait(barrier, n_dev - 1)
    each_peer(n_row, n_col, send_sum)
    parts[me] = sums[me]
    if last:
        each_peer(n_row, n_col if spread else 1, send_g)
        g_out[me if spread else row] = g[col if spread else 0]
    settle(parts, n_dev - 1, recv)
    spot = col if last else me
    f_out[spot] = f[me] - lse2(parts[...]) / (2 * SCALE)
    each_peer(1 if last else n_row, n_col, send_f)
    settle(parts, n_dev - 1, send)
    if last:
        others = (n_dev if spread else n_row) - 1
        settle(g_out, others, g_send)
        settle(g_out, others, g_recv)
    others = (n_col if last else n_dev) - 1
    settle(f_out, others, f_send)
    settle(f_out, others, f_recv)


def exchange(n_row, n_col, spread, last, sums, f, g):
    n_dev = n_row * n_col
    dma = pltpu.SemaphoreType.DMA
    sums, f = (a.reshape(n_dev, -1, 128) for a in (sums, f))
    amount = n_col if last else n_dev
    out = [jax.ShapeDtypeStruct((amount,) + f.shape[1:], f.dtype)]
    scratch = [VMEM(sums.shape, sums.dtype)] + [dma] * 4
    args = [sums, f]
    if last:
        fan = n_dev if spread else n_row
        g = g.reshape(n_col if spread else 1, -1, 128)
        out.append(jax.ShapeDtypeStruct((fan,) + g.shape[1:], g.dtype))
        scratch += [dma] * 2
        args.append(g)
    return pl.pallas_call(
        functools.partial(exchange_kernel, n_row, n_col, spread, last),
        out_shape=tuple(out),
        in_specs=[pl.BlockSpec(memory_space=VMEM)] * len(args),
        out_specs=(pl.BlockSpec(memory_space=VMEM),) * len(out),
        scratch_shapes=scratch,
        compiler_params=pltpu.CompilerParams(
            collective_id=2 if last else 1,
            has_side_effects=True,
            vmem_limit_bytes=32 * 1024 * 1024,
        ),
    )(*args)


def on_device(n_row, n_col, source_points, target_points, source_level, target_level, neighbours):
    group = target_points.shape[1] // BLOCK
    share = group // n_row
    spread = share % n_col == 0
    me_row, me_col = lax.axis_index("row"), lax.axis_index("col")
    start, length = me_row * share * BLOCK, share * BLOCK
    source = jnp.concatenate([source_points, source_level[None]], axis=0)
    target = jnp.concatenate(
        [
            lax.dynamic_slice_in_dim(target_points, start, length, 1),
            lax.dynamic_slice_in_dim(target_level, start, length, 0)[None],
        ],
        axis=0,
    )
    if spread:
        target = target.reshape(4, n_col, -1).transpose(1, 0, 2)
        part = share // n_col
        own = (
            jnp.arange(n_col)[:, None] * group
            + me_row * share + me_col * part + jnp.arange(part)[None, :]
        ).reshape(-1)
    else:
        target = target[None]
        own = me_col * group + me_row * share + jnp.arange(share)
    source, lists, target = gather(n_row, n_col, spread, source, neighbours, target)
    lists = lists.reshape(-1, lists.shape[-1])
    f, g = source[:, 3], target[:, 3]
    rows = lists.shape[0]
    cols = own.shape[0]
    capacity = rows * cols
    mask = jnp.any(lists[None] == own[:, None, None], axis=2).reshape(-1)
    order = jnp.arange(capacity)
    place = jnp.sum(jnp.where((order[None, :] <= order[:, None]) & mask[None, :], 1, 0), axis=1)
    count = jnp.max(place)
    slot = jnp.arange(-(-capacity // UNROLL) * UNROLL + 1)
    hit = mask[None, :] & (place[None, :] == slot[:, None] + 1)
    code = order % rows + (order // rows) * 65536
    pick = jnp.sum(jnp.where(hit, code[None, :], 0), axis=1)
    pairs = jnp.where(slot < count, pick, rows + cols * 65536)
    pairs = jnp.where(slot == slot.shape[0] - 1, count, pairs)

    for turn in range(ITERS):
        sums, g = sweep(pairs, source, f, target, g)
        if turn < ITERS - 1:
            (f,) = exchange(n_row, n_col, spread, False, sums, f, None)
    f, g = exchange(n_row, n_col, spread, True, sums, f, g)
    return f.reshape(-1), g.reshape(-1)


def solution(mesh):
    return jax.shard_map(
        functools.partial(on_device, mesh.shape["row"], mesh.shape["col"]),
        mesh=mesh,
        in_specs=(P(None, "row"), P(None, "col"), P("row"), P("col"), P("row", None)),
        out_specs=(P("row"), P("col")),
        check_vma=False,
    )
```
